128 devices in a mesh: dp: 8 (over x, z_hi), tensor: 16 (over z_lo, y, core).
Axes of the slice: x: 4, y: 4, z: 4 (z_hi: 2, z_lo: 2; z = z_hi * 2 + z_lo), core: 2. Of those that a mesh axis runs over, the one named last changes fastest.
Arguments:
- qkv_master: float32 [8, 1024, 5120], P('dp', 'tensor'), may hold values from -0.0625 to 0.0625
- qkv_moment1: float32 [8, 1024, 5120], P('dp', 'tensor'), may hold values from -6 to 6
- qkv_moment2: float32 [8, 1024, 5120], P('dp', 'tensor'), may hold values from 0.1 to 10
- qkv_grad: bfloat16 [8, 1024, 5120], P('dp', 'tensor'), may hold values from -6 to 6
- out_master: float32 [8, 1024, 4096], P('dp', 'tensor'), may hold values from -0.09375 to 0.09375
- out_moment1: float32 [8, 1024, 4096], P('dp', 'tensor'), may hold values from -6 to 6
- out_moment2: float32 [8, 1024, 4096], P('dp', 'tensor'), may hold values from 0.1 to 10
- out_grad: bfloat16 [8, 1024, 4096], P('dp', 'tensor'), may hold values from -6 to 6
- embed_table: bfloat16 [76032, 8, 1024], P('dp', None, 'tensor'), may hold values from -6 to 6
- norm_gain: float32 [8, 1024], P(None, 'tensor'), may hold values from 0.5 to 1.5
- token_ids: int32 [512, 4], P('dp'), may hold values from 0 to 76031, as said below
- lengths: int32 [512], P(('dp', 'tensor')), may hold values from 1 to 384, 98304 in all
- kv_cache: bfloat16 [512, 4, 384, 256], P(('dp', 'tensor')), may hold values from -6 to 6
Outputs:
- decoded: bfloat16 [512, 4, 8, 1024], P('dp', None, None, 'tensor')
- fresh_kv: bfloat16 [512, 4, 4, 256], P(('dp', 'tensor'))
- qkv_master_new: float32 [8, 1024, 5120], P('dp', 'tensor')
- qkv_moment1_new: float32 [8, 1024, 5120], P('dp', 'tensor')
- qkv_moment2_new: float32 [8, 1024, 5120], P('dp', 'tensor')
- out_master_new: float32 [8, 1024, 4096], P('dp', 'tensor')
- out_moment1_new: float32 [8, 1024, 4096], P('dp', 'tensor')
- out_moment2_new: float32 [8, 1024, 4096], P('dp', 'tensor')
The draws below stay inside these ranges and needn't reach their ends.
Inputs may be any that keep to these rules, and one draw needn't show every extreme that they name: `token_ids`: the vocabulary is 8 blocks of 9504 ids. Of the tokens of one decode group (each aligned run of 64 rows, all steps), exactly 64 fall in one block, chosen per group, and the rest are spread over the other blocks as evenly as possible. `lengths`: some row has exactly 384 cached tokens.
All inputs are finite; a program needn't handle non-finite values. No bound on the sum of `lengths` on one device may be relied on, other than what follows from the above.
Results may differ from the reference program's by a relative error of at most 0.0057.
Values may be sent and summed in bfloat16 or wider, within the bound.
No kernel may reach another device: no remote copies, remote signals or barrier semaphores. Data moves between devices by JAX's collectives and lax.ppermute only.
A program may use at most 128 MiB of HBM per device.

```python
import math
import jax
import jax.numpy as jnp
import numpy as np
from jax import lax

D = 8192
QH = 32
KVH = 4
HD = 128
VOCAB = 76032
ROW_DEV = 4
CTX = 384
STEPS = 4
QW = 4096
KW = 512
DW = 1024
ROWS = 512
N_DP = 8
N_TENSOR = 16


def draw_token_ids(key, part):
    key = jax.random.fold_in(key, 11)
    group_tokens = ROW_DEV * N_TENSOR * STEPS
    most_hits = 2 * group_tokens // N_DP
    shard_vocab = VOCAB // N_DP
    key_heavy, key_order, key_first, key_second = jax.random.split(key, 4)
    heavy = jax.random.randint(key_heavy, (N_DP, 1), 0, N_DP)
    slot = jnp.arange(group_tokens)[None, :]
    spread = jnp.maximum(slot - most_hits, 0) % max(N_DP - 1, 1)
    owner = jnp.where(slot < most_hits, heavy, (heavy + 1 + spread) % N_DP)
    order_keys = jax.random.split(key_order, N_DP)
    owner = jax.vmap(lambda one_key, one_row: jax.random.permutation(one_key, one_row))(order_keys, owner)
    first = jax.random.randint(key_first, (N_DP, group_tokens), 0, shard_vocab)
    second = jax.random.randint(key_second, (N_DP, group_tokens), 0, shard_vocab)
    inner = jnp.minimum(first, second)
    ids = owner * shard_vocab + inner
    return ids.reshape(ROWS, STEPS).astype(jnp.int32)


def steps_of(own_key, shape, pieces, low, high):
    level, own = 1.0, jax.random.fold_in(own_key, 6)
    for position, parts in pieces:
        draws = jnp.exp(jax.random.uniform(jax.random.fold_in(own, position), (parts,), jnp.float32, low / len(pieces), high / len(pieces)))
        level = level * jnp.repeat(draws, shape[position] // parts).reshape([-1 if axis == position else 1 for axis in range(len(shape))])
    return level


def profile(number_of, total, reach, lean):
    portions = [(1 << 20) // math.isqrt(grade ** lean) + 1 for grade in range(2, number_of + 1)]
    rest, holding = total - reach - (number_of - 1), [1] * (number_of - 1)
    while rest > 0:
        movable = [i for i in range(number_of - 1) if holding[i] < reach]
        pool, left = sum([portions[i] for i in movable]), rest
        for i in movable:
            more = min(reach - holding[i], max(1, left * portions[i] // pool), rest)
            holding[i] = holding[i] + more
            rest = rest - more
    return np.array([reach] + holding)


def uneven_parts(own_key, amount, total, reach, slope):
    if amount == 2:
        one = jax.random.randint(own_key, (), max(1, total - reach), min(reach, total - 1) + 1)
        return jnp.stack([one, total - one])
    sizes = jnp.asarray(profile(amount, total, reach, slope), jnp.int32)
    pairs = (amount - 1) // 2
    giver, sink = sizes[1:1 + 2 * pairs:2], sizes[2:2 + 2 * pairs:2]
    room = jnp.minimum(giver - 1, reach - sink)
    passed = jax.random.randint(jax.random.fold_in(own_key, 1), (pairs,), 0, 1 << 20) % (room + 1)
    sizes = sizes.at[1:1 + 2 * pairs:2].set(giver - passed).at[2:2 + 2 * pairs:2].set(sink + passed)
    return sizes[jax.random.permutation(jax.random.fold_in(own_key, 2), amount)]


def bell_draw(stream_key, dims, scale, reach, cuts=(), kind=jnp.bfloat16):
    level = steps_of(stream_key, dims, cuts, -0.22, 0.18) if cuts else 1.0
    array = jax.random.normal(stream_key, dims, jnp.float32) * scale * level
    return jnp.minimum(jnp.maximum(array, -reach), reach).astype(kind)


def setup_inputs(seed: int = 0) -> dict:
    seeds = jax.random.split(jax.random.key(seed), 14)
    return {
        "qkv_master": bell_draw(seeds[0], (N_DP, DW, QW + 2 * KW), D ** -0.5, 0.0625, ((0, 8), (1, 16)), jnp.float32),
        "qkv_moment1": bell_draw(seeds[1], (N_DP, DW, QW + 2 * KW), 1.0, 6.0, ((0, 8), (1, 16)), jnp.float32),
        "qkv_moment2": jnp.clip(jnp.exp(math.log(10.0) - 4.6051702 * jax.random.uniform(seeds[2], (N_DP, DW, QW + 2 * KW), jnp.float32) ** steps_of(seeds[2], (N_DP, DW, QW + 2 * KW), ((0, 8), (1, 16)), -0.2, 0.2)), 0.1, 10.0),
        "qkv_grad": bell_draw(seeds[3], (N_DP, DW, QW + 2 * KW), 1.0, 6.0, ((0, 8), (1, 16))),
        "out_master": bell_draw(seeds[4], (N_DP, DW, QW), QW ** -0.5, 0.09375, ((0, 8), (1, 16)), jnp.float32),
        "out_moment1": bell_draw(seeds[5], (N_DP, DW, QW), 1.0, 6.0, ((0, 8), (1, 16)), jnp.float32),
        "out_moment2": jnp.clip(jnp.exp(math.log(10.0) - 4.6051702 * jax.random.uniform(seeds[6], (N_DP, DW, QW), jnp.float32) ** steps_of(seeds[6], (N_DP, DW, QW), ((0, 8), (1, 16)), -0.2, 0.2)), 0.1, 10.0),
        "out_grad": bell_draw(seeds[7], (N_DP, DW, QW), 1.0, 6.0, ((0, 8), (1, 16))),
        "embed_table": bell_draw(seeds[8], (VOCAB, N_DP, DW), 1.0, 6.0, ((0, 8), (2, 16))),
        "norm_gain": jnp.clip(1.0 + 0.1 * jax.random.normal(seeds[9], (N_DP, DW), jnp.float32), 0.5, 1.5),
        "token_ids": draw_token_ids(jax.random.fold_in(seeds[13], 71), 0),
        "lengths": uneven_parts(seeds[11], ROWS, ROWS * CTX // 2, CTX, 1).astype(jnp.int32),
        "kv_cache": bell_draw(seeds[12], (ROWS, KVH, CTX, 2 * HD), 1.0, 6.0, ((0, 128),)),
    }


beta_first = 0.9
beta_second = 0.95
adam_epsilon = 1e-08
learn_rate = 0.002
decay_rate = 0.1
bias_first = 1.0 - 0.9 ** 50
bias_second = 1.0 - 0.95 ** 50
rope_base = 1000000.0
norm_epsilon = 1e-06

def adamw(master, moment_one, moment_two, gradient):
    grad_float = gradient.astype(jnp.float32)
    moment_one = beta_first * moment_one + (1.0 - beta_first) * grad_float
    moment_two = beta_second * moment_two + (1.0 - beta_second) * grad_float * grad_float
    stepped = moment_one / bias_first / (jnp.sqrt(moment_two / bias_second) + adam_epsilon)
    master = master - learn_rate * (stepped + decay_rate * master)
    return (master, moment_one, moment_two)

def rotate(values, positions):
    half_dim = values.shape[-1] // 2
    exponent = jnp.arange(half_dim).astype(jnp.float32) * (2.0 / values.shape[-1])
    freqs = jnp.power(jnp.float32(rope_base), -exponent)
    angles = positions.astype(jnp.float32)[..., None] * freqs
    cosine = jnp.cos(angles)[..., None, :]
    sine = jnp.sin(angles)[..., None, :]
    first_half = values[..., :half_dim]
    second_half = values[..., half_dim:]
    return jnp.concatenate([first_half * cosine - second_half * sine, second_half * cosine + first_half * sine], axis=-1)

def attend(queries, keys_new, values_new, cache, lengths):
    head_dim = queries.shape[-1]
    row_total, step_total = (queries.shape[0], queries.shape[1])
    scale = 1.0 / math.sqrt(head_dim)
    cache_keys = cache[..., :head_dim].astype(jnp.float32)
    cache_values = cache[..., head_dim:].astype(jnp.float32)
    query_float = queries.astype(jnp.float32)
    cache_scores = jnp.einsum('rsngd,rncd->rngsc', query_float, cache_keys) * scale
    new_scores = jnp.einsum('rsngd,rtnd->rngst', query_float, keys_new.astype(jnp.float32)) * scale
    cache_live = jnp.arange(cache.shape[2])[None, :] < lengths[:, None]
    cache_scores = jnp.where(cache_live[:, None, None, None, :], cache_scores, -jnp.inf)
    causal = jnp.arange(step_total)[:, None] >= jnp.arange(step_total)[None, :]
    new_scores = jnp.where(causal, new_scores, -jnp.inf)
    highest = jnp.maximum(lax.optimization_barrier(jnp.max(cache_scores, axis=-1)), lax.optimization_barrier(jnp.max(new_scores, axis=-1)))
    cache_exp = jnp.exp(cache_scores - highest[..., None])
    new_exp = jnp.exp(new_scores - highest[..., None])
    denom = lax.optimization_barrier(jnp.sum(cache_exp, axis=-1)) + lax.optimization_barrier(jnp.sum(new_exp, axis=-1))
    cache_weights = (cache_exp / denom[..., None]).astype(jnp.bfloat16)
    new_weights = (new_exp / denom[..., None]).astype(jnp.bfloat16)
    mixed = jnp.einsum('rngsc,rncd->rsngd', cache_weights.astype(jnp.float32), cache_values)
    mixed = mixed + jnp.einsum('rngst,rtnd->rsngd', new_weights.astype(jnp.float32), values_new.astype(jnp.float32))
    return mixed.astype(jnp.bfloat16).reshape(row_total, step_total, -1)

def reference(qkv_master, qkv_moment1, qkv_moment2, qkv_grad, out_master, out_moment1, out_moment2, out_grad, embed_table, norm_gain, token_ids, lengths, kv_cache):
    new_qkv = adamw(qkv_master, qkv_moment1, qkv_moment2, qkv_grad)
    new_out = adamw(out_master, out_moment1, out_moment2, out_grad)
    qkv_weights = new_qkv[0].astype(jnp.bfloat16).reshape(D, -1)
    out_weights = new_out[0].astype(jnp.bfloat16).reshape(D, QW)
    table = embed_table.reshape(VOCAB, D)
    hidden = jnp.take(table, token_ids, axis=0)
    hidden_float = hidden.astype(jnp.float32)
    inverse = lax.rsqrt(lax.optimization_barrier(jnp.mean(hidden_float * hidden_float, axis=-1, keepdims=True)) + norm_epsilon)
    normed = (hidden_float * inverse * norm_gain.reshape(D)).astype(jnp.bfloat16)
    projected = jnp.dot(normed.reshape(ROWS * STEPS, D), qkv_weights, preferred_element_type=jnp.float32)
    projected = projected.reshape(ROWS, STEPS, -1)
    query = projected[..., :QW].reshape(ROWS, STEPS, QH, HD)
    key = projected[..., QW:QW + KW].reshape(ROWS, STEPS, KVH, HD)
    value = projected[..., QW + KW:].reshape(ROWS, STEPS, KVH, HD)
    positions = lengths[:, None] + jnp.arange(STEPS).astype(jnp.int32)[None, :]
    query = rotate(query, positions).astype(jnp.bfloat16)
    key = rotate(key, positions).astype(jnp.bfloat16)
    value = value.astype(jnp.bfloat16)
    fresh_kv = jnp.concatenate([key, value], axis=-1)
    attended = attend(query.reshape(ROWS, STEPS, KVH, QH // KVH, HD), key, value, kv_cache, lengths)
    output = jnp.dot(attended.reshape(ROWS * STEPS, QW), out_weights.T, preferred_element_type=jnp.float32)
    decoded = (hidden_float + output.reshape(ROWS, STEPS, D)).astype(jnp.bfloat16).reshape(ROWS, STEPS, N_DP, DW)
    return (decoded, fresh_kv, new_qkv[0], new_qkv[1], new_qkv[2], new_out[0], new_out[1], new_out[2])
```

```python
import math

import jax
import jax.numpy as jnp
from jax import lax
from jax.experimental import pallas as pl
from jax.experimental.pallas import tpu as pltpu
from jax.sharding import PartitionSpec as P

D = 8192
QH = 32
KVH = 4
HD = 128
QW = 4096
KW = 512
VOCAB_DEV = 9504
SLOTS = 64
GROUPS = 8
TOK = 256
FEAT = 512
VCHUNK = 1920
HALF = 2560

beta_first = 0.9
beta_second = 0.95
adam_epsilon = 1e-08
learn_rate = 0.002
decay_rate = 0.1
bias_first = 1.0 - 0.9**50
bias_second = 1.0 - 0.95**50
rope_base = 1000000.0
norm_epsilon = 1e-06

f32 = jnp.float32
bf16 = jnp.bfloat16


def adamw(master, moment_one, moment_two, gradient):
    grad_float = gradient.astype(jnp.float32)
    moment_one = beta_first * moment_one + (1.0 - beta_first) * grad_float
    moment_two = beta_second * moment_two + (1.0 - beta_second) * grad_float * grad_float
    stepped = moment_one / bias_first / (jnp.sqrt(moment_two / bias_second) + adam_epsilon)
    master = master - learn_rate * (stepped + decay_rate * master)
    return (master, moment_one, moment_two)


def rotate(values, positions):
    half_dim = values.shape[-1] // 2
    exponent = jnp.arange(half_dim).astype(jnp.float32) * (2.0 / values.shape[-1])
    freqs = jnp.power(jnp.float32(rope_base), -exponent)
    angles = positions.astype(jnp.float32)[..., None] * freqs
    cosine = jnp.cos(angles)[..., None, :]
    sine = jnp.sin(angles)[..., None, :]
    first_half = values[..., :half_dim]
    second_half = values[..., half_dim:]
    return jnp.concatenate(
        [first_half * cosine - second_half * sine, second_half * cosine + first_half * sine],
        axis=-1,
    )


def attend(queries, keys_new, values_new, cache, lengths):
    head_dim = queries.shape[-1]
    row_total, step_total = (queries.shape[0], queries.shape[1])
    scale = 1.0 / math.sqrt(head_dim)
    cache_keys = cache[..., :head_dim]
    cache_values = cache[..., head_dim:]
    cache_scores = (
        jnp.einsum("rsngd,rncd->rngsc", queries, cache_keys, preferred_element_type=jnp.float32)
        * scale
    )
    new_scores = (
        jnp.einsum("rsngd,rtnd->rngst", queries, keys_new, preferred_element_type=jnp.float32)
        * scale
    )
    cache_live = jnp.arange(cache.shape[2])[None, :] < lengths[:, None]
    cache_scores = jnp.where(cache_live[:, None, None, None, :], cache_scores, -jnp.inf)
    causal = jnp.arange(step_total)[:, None] >= jnp.arange(step_total)[None, :]
    new_scores = jnp.where(causal, new_scores, -jnp.inf)
    highest = jnp.maximum(jnp.max(cache_scores, axis=-1), jnp.max(new_scores, axis=-1))
    cache_exp = jnp.exp(cache_scores - highest[..., None])
    new_exp = jnp.exp(new_scores - highest[..., None])
    denom = jnp.sum(cache_exp, axis=-1) + jnp.sum(new_exp, axis=-1)
    cache_weights = (cache_exp / denom[..., None]).astype(jnp.bfloat16)
    new_weights = (new_exp / denom[..., None]).astype(jnp.bfloat16)
    mixed = jnp.einsum(
        "rngsc,rncd->rsngd", cache_weights, cache_values, preferred_element_type=jnp.float32
    )
    mixed = mixed + jnp.einsum(
        "rngst,rtnd->rsngd", new_weights, values_new, preferred_element_type=jnp.float32
    )
    return mixed.astype(jnp.bfloat16).reshape(row_total, step_total, -1)


def iota(shape, axis):
    return lax.broadcasted_iota(jnp.int32, shape, axis)


def lower_triangle(size):
    return (iota((size, size), 0) <= iota((size, size), 1)).astype(bf16)


def lookup_kernel(ids_ref, table_ref, out_ref, acc_ref, pick_ref):
    step = pl.program_id(0)

    @pl.when(step == 0)
    def _():
        local = ids_ref[...]
        mine = (local >= 0) & (local < VOCAB_DEV)
        rank = jnp.dot(
            mine.astype(f32).astype(bf16), lower_triangle(TOK), preferred_element_type=f32
        )
        rank = jnp.where(mine, rank, 0.0)
        shifted = local.astype(f32) + 1.0
        for group in range(GROUPS):
            slot = iota((SLOTS, TOK), 0).astype(f32) + 1.0
            hit = rank[group : group + 1, :] == slot
            value = jnp.where(hit, shifted[group : group + 1, :], 0.0)
            pick = jnp.sum(value, axis=1, keepdims=True) - 1.0
            pick_ref[pl.ds(group * SLOTS, SLOTS), :] = jnp.broadcast_to(
                pick, (SLOTS, 128)
            ).astype(jnp.int32)
        acc_ref[...] = jnp.zeros_like(acc_ref)

    slots = GROUPS * SLOTS
    entry = iota((slots, VCHUNK), 1) + step * VCHUNK
    chosen = jnp.where(entry == pick_ref[:, 0:1], 1.0, 0.0).astype(bf16)
    dims = (((1,), (1,)), ((), ()))

    @pl.when(step < pl.num_programs(0) - 1)
    def _():
        acc_ref[...] += lax.dot_general(chosen, table_ref[...], dims, preferred_element_type=f32)

    @pl.when(step == pl.num_programs(0) - 1)
    def _():
        column = iota((FEAT, VCHUNK), 1) + step * VCHUNK
        block = jnp.where(column < VOCAB_DEV, table_ref[...], jnp.zeros((), bf16))
        total = acc_ref[...] + lax.dot_general(chosen, block, dims, preferred_element_type=f32)
        out_ref[...] = total.astype(bf16)


def lookup(local_ids, table):
    steps = pl.cdiv(VOCAB_DEV, VCHUNK)
    slots = GROUPS * SLOTS
    return pl.pallas_call(
        lookup_kernel,
        grid=(steps,),
        in_specs=[
            pl.BlockSpec((GROUPS, TOK), lambda i: (0, 0)),
            pl.BlockSpec((FEAT, VCHUNK), lambda i: (0, i)),
        ],
        out_specs=pl.BlockSpec((slots, FEAT), lambda i: (0, 0)),
        out_shape=jax.ShapeDtypeStruct((slots, FEAT), bf16),
        scratch_shapes=[pltpu.VMEM((slots, FEAT), f32), pltpu.VMEM((slots, 128), jnp.int32)],
        compiler_params=pltpu.CompilerParams(vmem_limit_bytes=40 * 2**20),
        cost_estimate=pl.CostEstimate(
            flops=2 * slots * FEAT * VOCAB_DEV,
            bytes_accessed=FEAT * VOCAB_DEV * 2,
            transcendentals=0,
        ),
        name="lookup",
    )(local_ids, table)


def arrange_kernel(ids_ref, slots_ref, gain_ref, order_ref, hidden_ref, scaled_ref, squares_ref):
    ids = jnp.broadcast_to(ids_ref[...], (GROUPS, TOK))
    low = iota((GROUPS, TOK), 0) * VOCAB_DEV
    owned = (ids >= low) & (ids < low + VOCAB_DEV)
    rank = jnp.dot(owned.astype(f32).astype(bf16), lower_triangle(TOK), preferred_element_type=f32)
    place = rank - 1.0 + (iota((GROUPS, TOK), 0) * SLOTS).astype(f32)
    place = jnp.sum(jnp.where(owned, place, 0.0), axis=0, keepdims=True)
    slots = GROUPS * SLOTS
    chosen = jnp.where(iota((slots, TOK), 0).astype(f32) == place, 1.0, 0.0).astype(bf16)
    hidden = lax.dot_general(
        chosen, slots_ref[...], (((0,), (0,)), ((), ())), preferred_element_type=f32
    )
    hidden_ref[...] = hidden.astype(bf16)
    squares = jnp.sum(hidden * hidden, axis=1, keepdims=True)
    squares_ref[...] = jnp.broadcast_to(squares, (TOK, 128)).astype(bf16)
    scaled = (hidden * gain_ref[...]).astype(bf16)
    order = jnp.where(iota((FEAT, FEAT), 0) == order_ref[...], 1.0, 0.0).astype(bf16)
    scaled_ref[...] = jnp.dot(scaled, order, preferred_element_type=f32).astype(bf16)


def arrange(ids_row, slots, gain, order):
    return pl.pallas_call(
        arrange_kernel,
        out_shape=(
            jax.ShapeDtypeStruct((TOK, FEAT), bf16),
            jax.ShapeDtypeStruct((TOK, FEAT), bf16),
            jax.ShapeDtypeStruct((TOK, 128), bf16),
        ),
        compiler_params=pltpu.CompilerParams(vmem_limit_bytes=40 * 2**20),
        name="arrange",
    )(ids_row, slots, gain, order)


def project_kernel(own_ref, pair_ref, squares_ref, *rest):
    shards, out_ref = rest[:-1], rest[-1]
    own = jnp.concatenate([shard[0:64, :] for shard in shards], axis=0)
    pair = jnp.concatenate([shard[64:128, :] for shard in shards], axis=0)
    total = jnp.dot(own_ref[...], own, preferred_element_type=f32)
    total = total + jnp.dot(pair_ref[...], pair, preferred_element_type=f32)
    out_ref[...] = total.astype(bf16)

    @pl.when(pl.program_id(0) == pl.num_programs(0) - 1)
    def _():
        out_ref[:, 256:384] = squares_ref[...]


def project(own, pair, squares, shards):
    width = HALF + 128
    steps = width // 384
    return pl.pallas_call(
        project_kernel,
        grid=(steps,),
        in_specs=[
            pl.BlockSpec((TOK, FEAT), lambda i: (0, 0)),
            pl.BlockSpec((TOK, FEAT), lambda i: (0, 0)),
            pl.BlockSpec((TOK, 128), lambda i: (0, 0)),
        ]
        + [pl.BlockSpec((128, 384), lambda i: (0, i)) for _ in shards],
        out_specs=pl.BlockSpec((TOK, 384), lambda i: (0, i)),
        out_shape=jax.ShapeDtypeStruct((TOK, width), bf16),
        compiler_params=pltpu.CompilerParams(vmem_limit_bytes=40 * 2**20),
        cost_estimate=pl.CostEstimate(
            flops=2 * TOK * 1024 * HALF, bytes_accessed=1024 * HALF * 2, transcendentals=0
        ),
        name="project",
    )(own, pair, squares, *shards)


def dp_permute(value, dx, dz):
    pairs = []
    for source in range(8):
        x, z = source // 2, source % 2
        pairs.append((source, ((x + dx) % 4) * 2 + (z ^ dz)))
    return lax.ppermute(value, "dp", pairs)


def tensor_permute(value, dz, dy, dc):
    pairs = []
    for source in range(16):
        z, y, c = source // 8, (source // 2) % 4, source % 2
        pairs.append((source, (z ^ dz) * 8 + ((y + dy) % 4) * 2 + (c ^ dc)))
    return lax.ppermute(value, "tensor", pairs)


def dp_gather(shard):
    other = dp_permute(shard, 0, 1)
    found = [shard] + [dp_permute(shard, step, 0) for step in (1, 3, 2)]
    return found + [other] + [dp_permute(other, step, 0) for step in (1, 3, 2)]


def on_device(
    qkv_master,
    qkv_moment1,
    qkv_moment2,
    qkv_grad,
    out_master,
    out_moment1,
    out_moment2,
    out_grad,
    embed_table,
    norm_gain,
    token_ids,
    lengths,
    kv_cache,
):
    group_rows, step_total = token_ids.shape
    my_group = lax.axis_index("dp")
    my_tensor = lax.axis_index("tensor")
    my_x, my_z = my_group // 2, my_group % 2
    my_core = my_tensor % 2

    ids_row = token_ids.reshape(1, TOK)
    all_ids = lax.all_to_all(
        jnp.broadcast_to(ids_row, (GROUPS, TOK)), "dp", split_axis=0, concat_axis=0, tiled=True
    )
    new_qkv = adamw(qkv_master, qkv_moment1, qkv_moment2, qkv_grad)
    qkv_local = new_qkv[0].astype(bf16)[0]
    kept = lax.dynamic_slice(qkv_local, (0, my_core * HALF), (64, HALF))
    given = lax.dynamic_slice(qkv_local, (0, (1 - my_core) * HALF), (64, HALF))
    qkv_shard = jnp.concatenate([kept, tensor_permute(given, 0, 0, 1)], axis=0)
    qkv_shards = dp_gather(qkv_shard)

    table = embed_table.transpose(1, 2, 0).reshape(FEAT, VOCAB_DEV)
    sent = lookup(all_ids - my_group * VOCAB_DEV, table)
    received = lax.all_to_all(
        sent.reshape(GROUPS, SLOTS, FEAT), "dp", split_axis=0, concat_axis=0, tiled=True
    ).reshape(GROUPS * SLOTS, FEAT)
    blocks = jnp.stack(
        [
            ((my_x + 4 - step) % 4) * 2 + (my_z + flip) % 2
            for flip in (0, 1)
            for step in (0, 1, 3, 2)
        ]
    )
    order = (blocks[:, None] * 64 + jnp.arange(64)[None, :]).reshape(1, FEAT).astype(jnp.int32)
    hidden, scaled, squares = arrange(ids_row, received, norm_gain.reshape(1, FEAT), order)
    scaled_pair = tensor_permute(scaled, 0, 0, 1)

    partial = project(scaled, scaled_pair, squares, qkv_shards)
    parts = lax.all_to_all(
        partial.reshape(16, 16, HALF + 128), "tensor", split_axis=0, concat_axis=0, tiled=True
    )
    summed = jnp.sum(parts.astype(f32).reshape(8, 2, 16, HALF + 128), axis=0)
    square_sum = summed[0, :, HALF] + summed[1, :, HALF]
    inverse = lax.rsqrt(square_sum / D + norm_epsilon)
    projected = jnp.concatenate([summed[0, :, :HALF], summed[1, :, :HALF]], axis=-1)
    projected = projected * inverse[:, None]

    own_tokens = 16
    own_rows = own_tokens // step_total
    projected = projected.reshape(own_rows, step_total, -1)
    query = projected[..., :QW].reshape(own_rows, step_total, QH, HD)
    key_new = projected[..., QW : QW + KW].reshape(own_rows, step_total, KVH, HD)
    value_new = projected[..., QW + KW :].reshape(own_rows, step_total, KVH, HD)
    positions = lengths[:, None] + jnp.arange(step_total)[None, :]
    query = rotate(query, positions).astype(bf16)
    key_new = rotate(key_new, positions).astype(bf16)
    value_new = value_new.astype(bf16)
    fresh_kv = jnp.concatenate([key_new, value_new], axis=-1)
    attended = attend(
        query.reshape(own_rows, step_total, KVH, QH // KVH, HD),
        key_new,
        value_new,
        kv_cache,
        lengths,
    )
    attended = attended.reshape(own_tokens, QW)

    new_out = adamw(out_master, out_moment1, out_moment2, out_grad)
    out_full = lax.all_gather(new_out[0].astype(bf16), "dp", axis=0, tiled=True).reshape(FEAT, QW)

    other = tensor_permute(attended, 1, 0, 0)
    both = jnp.stack([attended, other])
    quad = jnp.stack([both] + [tensor_permute(both, 0, step, 0) for step in (1, 2, 3)])
    everyone = jnp.stack([quad, tensor_permute(quad, 0, 0, 1)])
    everyone = everyone.reshape(2, 4, 2, 16, QW)
    tensor_z, tensor_y = my_tensor // 8, (my_tensor // 2) % 4
    heads = jnp.zeros((16, 16, QW), bf16)
    for core in range(2):
        for step in range(4):
            for flip in range(2):
                source = (
                    ((tensor_z + flip) % 2) * 8
                    + ((tensor_y + 4 - step) % 4) * 2
                    + (my_core + core) % 2
                )
                heads = lax.dynamic_update_slice(
                    heads, everyone[core, step, flip][None], (source, 0, 0)
                )
    output = lax.dot_general(
        heads.reshape(TOK, QW), out_full, (((1,), (1,)), ((), ())), preferred_element_type=f32
    )
    decoded = (hidden.astype(f32) + output).astype(bf16).reshape(group_rows, step_total, 8, 64)
    return (
        decoded,
        fresh_kv,
        new_qkv[0],
        new_qkv[1],
        new_qkv[2],
        new_out[0],
        new_out[1],
        new_out[2],
    )


def solution(mesh):
    return jax.shard_map(
        on_device,
        mesh=mesh,
        in_specs=(
            P("dp", "tensor", None),
            P("dp", "tensor", None),
            P("dp", "tensor", None),
            P("dp", "tensor", None),
            P("dp", "tensor", None),
            P("dp", "tensor", None),
            P("dp", "tensor", None),
            P("dp", "tensor", None),
            P("dp", None, "tensor"),
            P(None, "tensor"),
            P("dp", None),
            P(("dp", "tensor")),
            P(("dp", "tensor"), None, None, None),
        ),
        out_specs=(
            P("dp", None, None, "tensor"),
            P(("dp", "tensor"), None, None, None),
            P("dp", "tensor", None),
            P("dp", "tensor", None),
            P("dp", "tensor", None),
            P("dp", "tensor", None),
            P("dp", "tensor", None),
            P("dp", "tensor", None),
        ),
        check_vma=False,
    )
```

```python
import math

import jax
import jax.numpy as jnp
from jax import lax
from jax.experimental import pallas as pl
from jax.experimental.pallas import tpu as pltpu
from jax.sharding import PartitionSpec as P

D = 8192
QH = 32
KVH = 4
HD = 128
QW = 4096
KW = 512
VOCAB_DEV = 9504
SLOTS = 64
GROUPS = 8
TOK = 256
FEAT = 512
VCHUNK = 1920
HALF = 2560
COLS = 896
VMEM = 56 * 2**20

beta_first = 0.9
beta_second = 0.95
adam_epsilon = 1e-08
learn_rate = 0.002
decay_rate = 0.1
bias_first = 1.0 - 0.9**50
bias_second = 1.0 - 0.95**50
rope_base = 1000000.0
norm_epsilon = 1e-06

f32 = jnp.float32
bf16 = jnp.bfloat16


def adamw(master, moment_one, moment_two, gradient):
    grad_float = gradient.astype(jnp.float32)
    moment_one = beta_first * moment_one + (1.0 - beta_first) * grad_float
    moment_two = beta_second * moment_two + (1.0 - beta_second) * grad_float * grad_float
    stepped = moment_one / bias_first / (jnp.sqrt(moment_two / bias_second) + adam_epsilon)
    master = master - learn_rate * (stepped + decay_rate * master)
    return (master, moment_one, moment_two)


def rotate(values, positions):
    half_dim = values.shape[-1] // 2
    exponent = jnp.arange(half_dim).astype(jnp.float32) * (2.0 / values.shape[-1])
    freqs = jnp.power(jnp.float32(rope_base), -exponent)
    angles = positions.astype(jnp.float32)[..., None] * freqs
    cosine = jnp.cos(angles)[..., None, :]
    sine = jnp.sin(angles)[..., None, :]
    first_half = values[..., :half_dim]
    second_half = values[..., half_dim:]
    return jnp.concatenate(
        [first_half * cosine - second_half * sine, second_half * cosine + first_half * sine],
        axis=-1,
    )


def attend(queries, keys_new, values_new, cache, lengths):
    head_dim = queries.shape[-1]
    row_total, step_total = (queries.shape[0], queries.shape[1])
    scale = 1.0 / math.sqrt(head_dim)
    cache_keys = cache[..., :head_dim]
    cache_values = cache[..., head_dim:]
    cache_scores = (
        jnp.einsum("rsngd,rncd->rngsc", queries, cache_keys, preferred_element_type=jnp.float32)
        * scale
    )
    new_scores = (
        jnp.einsum("rsngd,rtnd->rngst", queries, keys_new, preferred_element_type=jnp.float32)
        * scale
    )
    cache_live = jnp.arange(cache.shape[2])[None, :] < lengths[:, None]
    cache_scores = jnp.where(cache_live[:, None, None, None, :], cache_scores, -jnp.inf)
    causal = jnp.arange(step_total)[:, None] >= jnp.arange(step_total)[None, :]
    new_scores = jnp.where(causal, new_scores, -jnp.inf)
    highest = jnp.maximum(jnp.max(cache_scores, axis=-1), jnp.max(new_scores, axis=-1))
    cache_exp = jnp.exp(cache_scores - highest[..., None])
    new_exp = jnp.exp(new_scores - highest[..., None])
    denom = jnp.sum(cache_exp, axis=-1) + jnp.sum(new_exp, axis=-1)
    cache_weights = (cache_exp / denom[..., None]).astype(jnp.bfloat16)
    new_weights = (new_exp / denom[..., None]).astype(jnp.bfloat16)
    mixed = jnp.einsum(
        "rngsc,rncd->rsngd", cache_weights, cache_values, preferred_element_type=jnp.float32
    )
    mixed = mixed + jnp.einsum(
        "rngst,rtnd->rsngd", new_weights, values_new, preferred_element_type=jnp.float32
    )
    return mixed.astype(jnp.bfloat16).reshape(row_total, step_total, -1)


def iota(shape, axis):
    return lax.broadcasted_iota(jnp.int32, shape, axis)


def lower_triangle(size):
    return (iota((size, size), 0) <= iota((size, size), 1)).astype(bf16)


def lookup_kernel(ids_ref, table_ref, out_ref, acc_ref, pick_ref):
    step = pl.program_id(0)

    @pl.when(step == 0)
    def _():
        local = ids_ref[...]
        mine = (local >= 0) & (local < VOCAB_DEV)
        rank = jnp.dot(
            mine.astype(f32).astype(bf16), lower_triangle(TOK), preferred_element_type=f32
        )
        rank = jnp.where(mine, rank, 0.0)
        shifted = local.astype(f32) + 1.0
        for group in range(GROUPS):
            slot = iota((SLOTS, TOK), 0).astype(f32) + 1.0
            hit = rank[group : group + 1, :] == slot
            value = jnp.where(hit, shifted[group : group + 1, :], 0.0)
            pick = jnp.sum(value, axis=1, keepdims=True) - 1.0
            pick_ref[pl.ds(group * SLOTS, SLOTS), :] = jnp.broadcast_to(
                pick, (SLOTS, 128)
            ).astype(jnp.int32)
        acc_ref[...] = jnp.zeros_like(acc_ref)

    slots = GROUPS * SLOTS
    entry = iota((slots, VCHUNK), 1) + step * VCHUNK
    chosen = jnp.where(entry == pick_ref[:, 0:1], 1.0, 0.0).astype(bf16)
    dims = (((1,), (1,)), ((), ()))

    @pl.when(step < pl.num_programs(0) - 1)
    def _():
        acc_ref[...] += lax.dot_general(chosen, table_ref[...], dims, preferred_element_type=f32)

    @pl.when(step == pl.num_programs(0) - 1)
    def _():
        column = iota((FEAT, VCHUNK), 1) + step * VCHUNK
        block = jnp.where(column < VOCAB_DEV, table_ref[...], jnp.zeros((), bf16))
        total = acc_ref[...] + lax.dot_general(chosen, block, dims, preferred_element_type=f32)
        out_ref[...] = total.astype(bf16)


def lookup(local_ids, table):
    steps = pl.cdiv(VOCAB_DEV, VCHUNK)
    slots = GROUPS * SLOTS
    return pl.pallas_call(
        lookup_kernel,
        grid=(steps,),
        in_specs=[
            pl.BlockSpec((GROUPS, TOK), lambda i: (0, 0)),
            pl.BlockSpec((FEAT, VCHUNK), lambda i: (0, i)),
        ],
        out_specs=pl.BlockSpec((slots, FEAT), lambda i: (0, 0)),
        out_shape=jax.ShapeDtypeStruct((slots, FEAT), bf16),
        scratch_shapes=[pltpu.VMEM((slots, FEAT), f32), pltpu.VMEM((slots, 128), jnp.int32)],
        compiler_params=pltpu.CompilerParams(vmem_limit_bytes=VMEM),
        cost_estimate=pl.CostEstimate(flops=2**20, bytes_accessed=2**18, transcendentals=0),
        name="lookup",
    )(local_ids, table)


def arrange_kernel(ids_ref, slots_ref, gain_ref, order_ref, hidden_ref, scaled_ref, squares_ref):
    ids = jnp.broadcast_to(ids_ref[...], (GROUPS, TOK))
    low = iota((GROUPS, TOK), 0) * VOCAB_DEV
    owned = (ids >= low) & (ids < low + VOCAB_DEV)
    rank = jnp.dot(owned.astype(f32).astype(bf16), lower_triangle(TOK), preferred_element_type=f32)
    place = rank - 1.0 + (iota((GROUPS, TOK), 0) * SLOTS).astype(f32)
    place = jnp.sum(jnp.where(owned, place, 0.0), axis=0, keepdims=True)
    slots = GROUPS * SLOTS
    chosen = jnp.where(iota((slots, TOK), 0).astype(f32) == place, 1.0, 0.0).astype(bf16)
    hidden = lax.dot_general(
        chosen, slots_ref[...], (((0,), (0,)), ((), ())), preferred_element_type=f32
    )
    hidden_ref[...] = hidden.astype(bf16)
    squares = jnp.sum(hidden * hidden, axis=1, keepdims=True)
    squares_ref[...] = jnp.broadcast_to(squares, (TOK, 128)).astype(bf16)
    scaled = (hidden * gain_ref[...]).astype(bf16)
    order = jnp.where(iota((FEAT, FEAT), 0) == order_ref[...], 1.0, 0.0).astype(bf16)
    scaled_ref[...] = jnp.dot(scaled, order, preferred_element_type=f32).astype(bf16)


def arrange(ids_row, slots, gain, order):
    return pl.pallas_call(
        arrange_kernel,
        out_shape=(
            jax.ShapeDtypeStruct((TOK, FEAT), bf16),
            jax.ShapeDtypeStruct((TOK, FEAT), bf16),
            jax.ShapeDtypeStruct((TOK, 128), bf16),
        ),
        compiler_params=pltpu.CompilerParams(vmem_limit_bytes=VMEM),
        name="arrange",
    )(ids_row, slots, gain, order)


def project_kernel(own_ref, pair_ref, squares_ref, *rest):
    (
        first,
        first_z,
        from_behind,
        from_ahead,
        far,
        far_z,
        second,
        second_z,
        behind,
        ahead,
        far_second,
        near_z,
        far_second_z,
        out_ref,
    ) = rest
    own = jnp.concatenate(
        [
            first[...],
            from_behind[0:64, :],
            from_ahead[0:64, :],
            far[...],
            first_z[...],
            from_behind[64:128, :],
            from_ahead[64:128, :],
            far_z[...],
        ],
        axis=0,
    )
    pair = jnp.concatenate(
        [
            second[...],
            behind[...],
            ahead[...],
            far_second[...],
            second_z[...],
            near_z[...],
            far_second_z[...],
        ],
        axis=0,
    )
    total = jnp.dot(own_ref[...], own, preferred_element_type=f32)
    total = total + jnp.dot(pair_ref[...], pair, preferred_element_type=f32)
    out_ref[...] = total.astype(bf16)

    @pl.when(pl.program_id(0) == pl.num_programs(0) - 1)
    def _():
        out_ref[:, COLS - 128 : COLS] = squares_ref[...]


def project(own, pair, squares, shards):
    width = HALF + 128
    return pl.pallas_call(
        project_kernel,
        grid=(width // COLS,),
        in_specs=[
            pl.BlockSpec((TOK, FEAT), lambda i: (0, 0)),
            pl.BlockSpec((TOK, FEAT), lambda i: (0, 0)),
            pl.BlockSpec((TOK, 128), lambda i: (0, 0)),
        ]
        + [pl.BlockSpec((shard.shape[0], COLS), lambda i: (0, i)) for shard in shards],
        out_specs=pl.BlockSpec((TOK, COLS), lambda i: (0, i)),
        out_shape=jax.ShapeDtypeStruct((TOK, width), bf16),
        compiler_params=pltpu.CompilerParams(vmem_limit_bytes=VMEM),
        cost_estimate=pl.CostEstimate(
            flops=2 * TOK * 1024 * HALF, bytes_accessed=1024 * HALF * 2, transcendentals=0
        ),
        name="project",
    )(own, pair, squares, *shards)


OUT_PIECES = (
    (0, 0, 64, 0, 0),
    (1, 0, 64, 1, 0),
    (2, 0, 64, 2, 0),
    (4, 64, 32, 3, 0),
    (5, 64, 32, 3, 32),
    (3, 0, 64, 4, 0),
    (4, 0, 64, 5, 0),
    (5, 0, 64, 6, 0),
    (6, 0, 32, 7, 0),
    (7, 0, 32, 7, 32),
)


def collect_kernel(blocks_ref, *rest):
    pieces, (out_ref, sems) = rest[:8], rest[8:]
    copies = []
    for piece, first, count, block, offset in OUT_PIECES:
        row = pl.multiple_of(blocks_ref[block] * 64 + offset, 32)
        copies.append(
            pltpu.make_async_copy(
                pieces[piece].at[pl.ds(first, count), :],
                out_ref.at[pl.ds(row, count), :],
                sems.at[len(copies)],
            )
        )
    for copy in copies:
        copy.start()
    for copy in copies:
        copy.wait()


def collect(blocks, pieces):
    anywhere = pl.BlockSpec(memory_space=pl.ANY)
    return pl.pallas_call(
        collect_kernel,
        in_specs=[pl.BlockSpec(memory_space=pltpu.SMEM)] + [anywhere] * 8,
        out_specs=pl.BlockSpec(memory_space=pltpu.VMEM),
        out_shape=jax.ShapeDtypeStruct((FEAT, QW), bf16),
        scratch_shapes=[pltpu.SemaphoreType.DMA((len(OUT_PIECES),))],
        compiler_params=pltpu.CompilerParams(vmem_limit_bytes=16 * 2**20),
        cost_estimate=pl.CostEstimate(flops=0, bytes_accessed=2**18, transcendentals=0),
        name="collect",
    )(blocks, *pieces)


def dp_permute(value, dx, dz):
    pairs = []
    for source in range(8):
        x, z = source // 2, source % 2
        pairs.append((source, ((x + dx) % 4) * 2 + (z ^ dz)))
    return lax.ppermute(value, "dp", pairs)


def tensor_permute(value, dz, dy, dc):
    pairs = []
    for source in range(16):
        z, y, c = source // 8, (source // 2) % 4, source % 2
        pairs.append((source, (z ^ dz) * 8 + ((y + dy) % 4) * 2 + (c ^ dc)))
    return lax.ppermute(value, "tensor", pairs)


def tied(value, *after):
    return lax.optimization_barrier((value,) + after)[0]


def gather_output(shard, after):
    other = dp_permute(shard, 0, 1)
    shard = tied(shard, *after)
    behind = dp_permute(shard, 1, 0)
    ahead = dp_permute(shard, 3, 0)
    from_behind = dp_permute(jnp.concatenate([other, behind[:32]], axis=0), 1, 0)
    from_ahead = dp_permute(jnp.concatenate([other, ahead[32:]], axis=0), 3, 0)
    far_low = dp_permute(from_behind[:32], 1, 0)
    far_high = dp_permute(from_ahead[32:64], 3, 0)
    return shard, behind, ahead, other, from_behind, from_ahead, far_low, far_high


def on_device(
    qkv_master,
    qkv_moment1,
    qkv_moment2,
    qkv_grad,
    out_master,
    out_moment1,
    out_moment2,
    out_grad,
    embed_table,
    norm_gain,
    token_ids,
    lengths,
    kv_cache,
):
    group_rows, step_total = token_ids.shape
    my_group = lax.axis_index("dp")
    my_tensor = lax.axis_index("tensor")
    my_x, my_z = my_group // 2, my_group % 2
    my_core = my_tensor % 2

    ids_row = token_ids.reshape(1, TOK)
    new_qkv = adamw(qkv_master, qkv_moment1, qkv_moment2, qkv_grad)
    qkv_local = new_qkv[0].astype(bf16)[0]
    kept = lax.dynamic_slice(qkv_local, (0, my_core * HALF), (64, HALF))
    given = lax.dynamic_slice(qkv_local, (0, (1 - my_core) * HALF), (64, HALF))
    taken = tensor_permute(given, 0, 0, 1)
    ids_sent = tied(jnp.broadcast_to(ids_row, (GROUPS, TOK)), taken)
    all_ids = lax.all_to_all(ids_sent, "dp", split_axis=0, concat_axis=0, tiled=True)

    kept_z = dp_permute(kept, 0, 1)
    taken_z = dp_permute(taken, 0, 1)
    behind = dp_permute(taken, 1, 0)
    ahead = dp_permute(taken, 3, 0)
    up = jnp.concatenate([kept, kept_z, behind[:32]], axis=0)
    down = jnp.concatenate([kept, kept_z, ahead[32:]], axis=0)
    near = jnp.concatenate([behind, ahead], axis=0)
    from_behind = dp_permute(up, 1, 0)
    from_ahead = dp_permute(down, 3, 0)
    near_z = dp_permute(near, 0, 1)
    far = dp_permute(from_behind[:64], 1, 0)
    far_z = dp_permute(from_ahead[64:128], 3, 0)
    far_taken = jnp.concatenate([from_behind[128:160], from_ahead[128:160]], axis=0)
    far_taken_z = dp_permute(far_taken, 0, 1)
    qkv_pieces = (
        kept,
        kept_z,
        from_behind,
        from_ahead,
        far,
        far_z,
        taken,
        taken_z,
        behind,
        ahead,
        far_taken,
        near_z,
        far_taken_z,
    )
    new_out = adamw(out_master, out_moment1, out_moment2, out_grad)
    out_local = new_out[0].astype(bf16)[0]

    table = embed_table.transpose(1, 2, 0).reshape(FEAT, VOCAB_DEV)
    local_ids = tied(all_ids - my_group * VOCAB_DEV, up, down, near)
    sent = lookup(local_ids, table)
    received = lax.all_to_all(
        sent.reshape(GROUPS, SLOTS, FEAT), "dp", split_axis=0, concat_axis=0, tiled=True
    ).reshape(GROUPS * SLOTS, FEAT)
    received = tied(received, far_taken, out_local)
    blocks = jnp.stack(
        [
            ((my_x + 4 - step) % 4) * 2 + (my_z + flip) % 2
            for flip in (0, 1)
            for step in (0, 1, 3, 2)
        ]
    )
    order = (blocks[:, None] * 64 + jnp.arange(64)[None, :]).reshape(1, FEAT).astype(jnp.int32)
    hidden, scaled, squares = arrange(ids_row, received, norm_gain.reshape(1, FEAT), order)
    scaled_pair = tensor_permute(scaled, 0, 0, 1)

    partial = project(scaled, scaled_pair, squares, qkv_pieces)
    parts = lax.all_to_all(
        partial.reshape(16, 16, HALF + 128), "tensor", split_axis=0, concat_axis=0, tiled=True
    )
    summed = jnp.sum(parts.astype(f32).reshape(8, 2, 16, HALF + 128), axis=0)
    square_sum = summed[0, :, HALF] + summed[1, :, HALF]
    inverse = lax.rsqrt(square_sum / D + norm_epsilon)
    projected = jnp.concatenate([summed[0, :, :HALF], summed[1, :, :HALF]], axis=-1)
    projected = projected * inverse[:, None]

    own_tokens = 16
    own_rows = own_tokens // step_total
    projected = projected.reshape(own_rows, step_total, -1)
    query = projected[..., :QW].reshape(own_rows, step_total, QH, HD)
    key_new = projected[..., QW : QW + KW].reshape(own_rows, step_total, KVH, HD)
    value_new = projected[..., QW + KW :].reshape(own_rows, step_total, KVH, HD)
    positions = lengths[:, None] + jnp.arange(step_total)[None, :]
    query = rotate(query, positions).astype(bf16)
    key_new = rotate(key_new, positions).astype(bf16)
    value_new = value_new.astype(bf16)
    fresh_kv = jnp.concatenate([key_new, value_new], axis=-1)
    attended = attend(
        query.reshape(own_rows, step_total, KVH, QH // KVH, HD),
        key_new,
        value_new,
        kv_cache,
        lengths,
    )
    attended = attended.reshape(own_tokens, QW)

    out_pieces = gather_output(out_local, (far, far_z))

    other = tensor_permute(attended, 1, 0, 0)
    both = jnp.stack([attended, other])
    quad = jnp.stack([both] + [tensor_permute(both, 0, step, 0) for step in (1, 2, 3)])
    away = tensor_permute(quad, 0, 0, 1)
    tensor_z, tensor_y = my_tensor // 8, (my_tensor // 2) % 4
    heads = jnp.zeros((16, 16, QW), bf16)
    for core, found in enumerate((quad, away)):
        for step in range(4):
            for flip in range(2):
                source = (
                    ((tensor_z + flip) % 2) * 8
                    + ((tensor_y + 4 - step) % 4) * 2
                    + (my_core + core) % 2
                )
                heads = lax.dynamic_update_slice(heads, found[step, flip][None], (source, 0, 0))
    output = lax.dot_general(
        heads.reshape(TOK, QW),
        collect(blocks.astype(jnp.int32), out_pieces),
        (((1,), (1,)), ((), ())),
        preferred_element_type=f32,
    )
    decoded = (hidden.astype(f32) + output).astype(bf16).reshape(group_rows, step_total, 8, 64)
    return (
        decoded,
        fresh_kv,
        new_qkv[0],
        new_qkv[1],
        new_qkv[2],
        new_out[0],
        new_out[1],
        new_out[2],
    )


def solution(mesh):
    return jax.shard_map(
        on_device,
        mesh=mesh,
        in_specs=(
            P("dp", "tensor", None),
            P("dp", "tensor", None),
            P("dp", "tensor", None),
            P("dp", "tensor", None),
            P("dp", "tensor", None),
            P("dp", "tensor", None),
            P("dp", "tensor", None),
            P("dp", "tensor", None),
            P("dp", None, "tensor"),
            P(None, "tensor"),
            P("dp", None),
            P(("dp", "tensor")),
            P(("dp", "tensor"), None, None, None),
        ),
        out_specs=(
            P("dp", None, None, "tensor"),
            P(("dp", "tensor"), None, None, None),
            P("dp", "tensor", None),
            P("dp", "tensor", None),
            P("dp", "tensor", None),
            P("dp", "tensor", None),
            P("dp", "tensor", None),
            P("dp", "tensor", None),
        ),
        check_vma=False,
    )
```

```python
import math

import jax
import jax.numpy as jnp
from jax import lax
from jax.experimental import pallas as pl
from jax.experimental.pallas import tpu as pltpu
from jax.sharding import PartitionSpec as P

D = 8192
QH = 32
KVH = 4
HD = 128
QW = 4096
KW = 512
VOCAB_DEV = 9504
SLOTS = 64
GROUPS = 8
TOK = 256
FEAT = 512
VCHUNK = 3200
HALF = 2560
COLS = 896
VMEM = 56 * 2**20

beta_first = 0.9
beta_second = 0.95
adam_epsilon = 1e-08
learn_rate = 0.002
decay_rate = 0.1
bias_first = 1.0 - 0.9**50
bias_second = 1.0 - 0.95**50
rope_base = 1000000.0
norm_epsilon = 1e-06

f32 = jnp.float32
bf16 = jnp.bfloat16


def adamw(master, moment_one, moment_two, gradient):
    grad_float = gradient.astype(jnp.float32)
    moment_one = beta_first * moment_one + (1.0 - beta_first) * grad_float
    moment_two = beta_second * moment_two + (1.0 - beta_second) * grad_float * grad_float
    stepped = moment_one / bias_first / (jnp.sqrt(moment_two / bias_second) + adam_epsilon)
    master = master - learn_rate * (stepped + decay_rate * master)
    return (master, moment_one, moment_two)


def iota(shape, axis):
    return lax.broadcasted_iota(jnp.int32, shape, axis)


def lower_triangle(size):
    return (iota((size, size), 0) <= iota((size, size), 1)).astype(bf16)


def lookup_kernel(ids_ref, table_ref, out_ref, acc_ref, pick_ref):
    step = pl.program_id(0)

    @pl.when(step == 0)
    def _():
        local = ids_ref[:, 0, :] - lax.axis_index("dp") * VOCAB_DEV
        mine = (local >= 0) & (local < VOCAB_DEV)
        rank = jnp.dot(
            mine.astype(f32).astype(bf16), lower_triangle(TOK), preferred_element_type=f32
        )
        rank = jnp.where(mine, rank, 0.0)
        shifted = local.astype(f32) + 1.0
        for group in range(GROUPS):
            slot = iota((SLOTS, TOK), 0).astype(f32) + 1.0
            hit = rank[group : group + 1, :] == slot
            value = jnp.where(hit, shifted[group : group + 1, :], 0.0)
            pick = jnp.sum(value, axis=1, keepdims=True) - 1.0
            pick_ref[pl.ds(group * SLOTS, SLOTS), :] = jnp.broadcast_to(
                pick, (SLOTS, 128)
            ).astype(jnp.int32)
        acc_ref[...] = jnp.zeros_like(acc_ref)

    slots = GROUPS * SLOTS
    entry = iota((slots, VCHUNK), 1) + step * VCHUNK
    chosen = jnp.where(entry == pick_ref[:, 0:1], 1.0, 0.0).astype(bf16)
    dims = (((1,), (1,)), ((), ()))

    @pl.when(step < pl.num_programs(0) - 1)
    def _():
        acc_ref[...] += lax.dot_general(chosen, table_ref[...], dims, preferred_element_type=f32)

    @pl.when(step == pl.num_programs(0) - 1)
    def _():
        column = iota((FEAT, VCHUNK), 1) + step * VCHUNK
        block = jnp.where(column < VOCAB_DEV, table_ref[...], jnp.zeros((), bf16))
        total = acc_ref[...] + lax.dot_general(chosen, block, dims, preferred_element_type=f32)
        out_ref[...] = total.astype(bf16)


def lookup(all_ids, table):
    steps = pl.cdiv(VOCAB_DEV, VCHUNK)
    slots = GROUPS * SLOTS
    return pl.pallas_call(
        lookup_kernel,
        grid=(steps,),
        in_specs=[
            pl.BlockSpec((GROUPS, 1, TOK), lambda i: (0, 0, 0)),
            pl.BlockSpec((FEAT, VCHUNK), lambda i: (0, i)),
        ],
        out_specs=pl.BlockSpec((slots, FEAT), lambda i: (0, 0)),
        out_shape=jax.ShapeDtypeStruct((slots, FEAT), bf16),
        scratch_shapes=[pltpu.VMEM((slots, FEAT), f32), pltpu.VMEM((slots, 128), jnp.int32)],
        compiler_params=pltpu.CompilerParams(vmem_limit_bytes=VMEM),
        cost_estimate=pl.CostEstimate(flops=3 * 10**10, bytes_accessed=10**7, transcendentals=0),
        name="lookup",
    )(all_ids, table)


def arrange_kernel(ids_ref, slots_ref, gain_ref, hidden_ref, scaled_ref, squares_ref):
    group = lax.axis_index("dp")
    ids = jnp.where(iota((GROUPS, TOK), 0) == group, ids_ref[:, 0, :], 0)
    ids = jnp.broadcast_to(jnp.sum(ids, axis=0, keepdims=True), (GROUPS, TOK))
    low = iota((GROUPS, TOK), 0) * VOCAB_DEV
    owned = (ids >= low) & (ids < low + VOCAB_DEV)
    rank = jnp.dot(owned.astype(f32).astype(bf16), lower_triangle(TOK), preferred_element_type=f32)
    place = rank - 1.0 + (iota((GROUPS, TOK), 0) * SLOTS).astype(f32)
    place = jnp.sum(jnp.where(owned, place, 0.0), axis=0, keepdims=True)
    slots = GROUPS * SLOTS
    chosen = jnp.where(iota((slots, TOK), 0).astype(f32) == place, 1.0, 0.0).astype(bf16)
    hidden = lax.dot_general(
        chosen, slots_ref[...], (((0,), (0,)), ((), ())), preferred_element_type=f32
    )
    hidden_ref[...] = hidden.astype(bf16)
    squares = jnp.sum(hidden * hidden, axis=1, keepdims=True)
    squares_ref[...] = jnp.broadcast_to(squares, (TOK, 128)).astype(bf16)
    gain = jnp.concatenate([gain_ref[block : block + 1, :] for block in range(8)], axis=1)
    scaled = (hidden * gain).astype(bf16)
    lane = iota((1, FEAT), 1)
    step = (lane // 64) % 4
    step = jnp.where(step == 2, 3, jnp.where(step == 3, 2, step))
    block = ((group // 2 + 4 - step) % 4) * 2 + (group % 2 + lane // 256) % 2
    order = block * 64 + lane % 64
    order = jnp.where(iota((FEAT, FEAT), 0) == order, 1.0, 0.0).astype(bf16)
    scaled_ref[...] = jnp.dot(scaled, order, preferred_element_type=f32).astype(bf16)


def arrange(all_ids, slots, gain):
    return pl.pallas_call(
        arrange_kernel,
        out_shape=(
            jax.ShapeDtypeStruct((TOK, FEAT), bf16),
            jax.ShapeDtypeStruct((TOK, FEAT), bf16),
            jax.ShapeDtypeStruct((TOK, 128), bf16),
        ),
        compiler_params=pltpu.CompilerParams(vmem_limit_bytes=VMEM),
        name="arrange",
    )(all_ids, slots, gain)


def project_kernel(own_ref, pair_ref, squares_ref, *rest):
    (
        first,
        first_z,
        from_behind,
        from_ahead,
        far,
        far_z,
        second,
        second_z,
        behind,
        ahead,
        far_second,
        near_z,
        far_second_z,
        out_ref,
    ) = rest
    own = jnp.concatenate(
        [
            first[...],
            from_behind[0:64, :],
            from_ahead[0:64, :],
            far[...],
            first_z[...],
            from_behind[64:128, :],
            from_ahead[64:128, :],
            far_z[...],
        ],
        axis=0,
    )
    pair = jnp.concatenate(
        [
            second[...],
            behind[...],
            ahead[...],
            far_second[...],
            second_z[...],
            near_z[...],
            far_second_z[...],
        ],
        axis=0,
    )
    total = jnp.dot(own_ref[...], own, preferred_element_type=f32)
    total = total + jnp.dot(pair_ref[...], pair, preferred_element_type=f32)
    out_ref[...] = total.astype(bf16)

    @pl.when(pl.program_id(0) == pl.num_programs(0) - 1)
    def _():
        out_ref[:, COLS - 128 : COLS] = squares_ref[...]


def project(own, pair, squares, shards):
    width = HALF + 128
    return pl.pallas_call(
        project_kernel,
        grid=(width // COLS,),
        in_specs=[
            pl.BlockSpec((TOK, FEAT), lambda i: (0, 0)),
            pl.BlockSpec((TOK, FEAT), lambda i: (0, 0)),
            pl.BlockSpec((TOK, 128), lambda i: (0, 0)),
        ]
        + [pl.BlockSpec((shard.shape[0], COLS), lambda i: (0, i)) for shard in shards],
        out_specs=pl.BlockSpec((TOK, COLS), lambda i: (0, i)),
        out_shape=jax.ShapeDtypeStruct((TOK, width), bf16),
        compiler_params=pltpu.CompilerParams(vmem_limit_bytes=VMEM),
        cost_estimate=pl.CostEstimate(
            flops=2 * TOK * 1024 * HALF, bytes_accessed=1024 * HALF * 2, transcendentals=0
        ),
        name="project",
    )(own, pair, squares, *shards)


def attend_kernel(
    lengths_ref, parts_ref, cos_ref, sin_ref, cache_ref, out_ref, fresh_ref, proj_ref
):
    head = pl.program_id(0)

    @pl.when(head == 0)
    def _():
        sums = []
        for core in range(2):
            total = parts_ref[core].astype(f32)
            for chip in range(1, 8):
                total = total + parts_ref[2 * chip + core].astype(f32)
            sums.append(total)
        squares = sums[0][:, HALF : HALF + 1] + sums[1][:, HALF : HALF + 1]
        inverse = lax.rsqrt(squares * (1.0 / D) + norm_epsilon)
        for core in range(2):
            proj_ref[:, core * HALF : (core + 1) * HALF] = sums[core][:, :HALF] * inverse

    cosine, sine = cos_ref[...], sin_ref[...]

    def turned(values):
        return (values * cosine + pltpu.roll(values, 64, 1) * sine).astype(bf16)

    def columns(first):
        return proj_ref[:, pl.ds(pl.multiple_of(first, 128), 128)]

    query = jnp.concatenate(
        [turned(columns(head * 1024 + group * 128)) for group in range(8)], axis=0
    )
    key_new = turned(columns(QW + head * 128))
    value_new = columns(QW + KW + head * 128).astype(bf16)
    fresh_ref[:, 0:128] = key_new
    fresh_ref[:, 128:256] = value_new

    scale = 1.0 / math.sqrt(HD)
    across = (((1,), (1,)), ((), ()))
    context = cache_ref.shape[2]
    token = iota((128, context), 0) % 16
    place = iota((128, context), 1)
    scores = []
    for row in range(4):
        score = (
            lax.dot_general(query, cache_ref[row, 0, :, :HD], across, preferred_element_type=f32)
            * scale
        )
        live = (token // 4 == row) & (place < lengths_ref[row])
        scores.append(jnp.where(live, score, -jnp.inf))
    score = lax.dot_general(query, key_new, across, preferred_element_type=f32) * scale
    asking, asked = iota((128, 16), 0) % 16, iota((128, 16), 1)
    live = (asking // 4 == asked // 4) & (asking % 4 >= asked % 4)
    scores.append(jnp.where(live, score, -jnp.inf))
    highest = jnp.max(scores[4], axis=1, keepdims=True)
    for score in scores[:4]:
        highest = jnp.maximum(highest, jnp.max(score, axis=1, keepdims=True))
    raised = [jnp.exp(score - highest) for score in scores]
    denom = jnp.sum(raised[4], axis=1, keepdims=True)
    for part in raised[:4]:
        denom = denom + jnp.sum(part, axis=1, keepdims=True)
    share = 1.0 / denom
    mixed = jnp.dot((raised[4] * share).astype(bf16), value_new, preferred_element_type=f32)
    for row in range(4):
        mixed = mixed + jnp.dot(
            (raised[row] * share).astype(bf16),
            cache_ref[row, 0, :, HD:],
            preferred_element_type=f32,
        )
    for group in range(8):
        out_ref[:, group * 128 : (group + 1) * 128] = mixed[group * 16 : (group + 1) * 16].astype(
            bf16
        )


def attend(lengths, parts, cosine, sine, cache):
    rows, heads, context, width = cache.shape
    return pl.pallas_call(
        attend_kernel,
        grid=(heads,),
        in_specs=[
            pl.BlockSpec(memory_space=pltpu.SMEM),
            pl.BlockSpec((16, 16, HALF + 128), lambda n: (0, 0, 0)),
            pl.BlockSpec((16, HD), lambda n: (0, 0)),
            pl.BlockSpec((16, HD), lambda n: (0, 0)),
            pl.BlockSpec((rows, 1, context, width), lambda n: (0, n, 0, 0)),
        ],
        out_specs=(
            pl.BlockSpec((16, 1024), lambda n: (0, n)),
            pl.BlockSpec((16, 256), lambda n: (0, n)),
        ),
        out_shape=(
            jax.ShapeDtypeStruct((16, QW), bf16),
            jax.ShapeDtypeStruct((16, 2 * KW), bf16),
        ),
        scratch_shapes=[pltpu.VMEM((16, 2 * HALF), f32)],
        compiler_params=pltpu.CompilerParams(vmem_limit_bytes=VMEM),
        name="attend",
    )(lengths, parts, cosine, sine, cache)


def angles_of(lengths, step_total):
    half_dim = HD // 2
    exponent = jnp.arange(half_dim).astype(f32) * (2.0 / HD)
    freqs = jnp.power(f32(rope_base), -exponent)
    positions = (lengths[:, None] + jnp.arange(step_total)[None, :]).reshape(-1)
    angles = positions.astype(f32)[:, None] * freqs
    cosine, sine = jnp.cos(angles), jnp.sin(angles)
    return jnp.concatenate([cosine, cosine], axis=1), jnp.concatenate([-sine, sine], axis=1)


OUT_PIECES = (
    (0, 0, 64, 0, 0),
    (1, 0, 64, 1, 0),
    (2, 0, 64, 2, 0),
    (4, 64, 32, 3, 0),
    (5, 64, 32, 3, 32),
    (3, 0, 64, 4, 0),
    (4, 0, 64, 5, 0),
    (5, 0, 64, 6, 0),
    (6, 0, 32, 7, 0),
    (7, 0, 32, 7, 32),
)


def collect_kernel(blocks_ref, *rest):
    pieces, (out_ref, sems) = rest[:8], rest[8:]
    copies = []
    for piece, first, count, block, offset in OUT_PIECES:
        row = pl.multiple_of(blocks_ref[block] * 64 + offset, 32)
        copies.append(
            pltpu.make_async_copy(
                pieces[piece].at[pl.ds(first, count), :],
                out_ref.at[pl.ds(row, count), :],
                sems.at[len(copies)],
            )
        )
    for copy in copies:
        copy.start()
    for copy in copies:
        copy.wait()


def collect(blocks, pieces):
    anywhere = pl.BlockSpec(memory_space=pl.ANY)
    return pl.pallas_call(
        collect_kernel,
        in_specs=[pl.BlockSpec(memory_space=pltpu.SMEM)] + [anywhere] * 8,
        out_specs=pl.BlockSpec(memory_space=pltpu.VMEM),
        out_shape=jax.ShapeDtypeStruct((FEAT, QW), bf16),
        scratch_shapes=[pltpu.SemaphoreType.DMA((len(OUT_PIECES),))],
        compiler_params=pltpu.CompilerParams(vmem_limit_bytes=16 * 2**20),
        cost_estimate=pl.CostEstimate(flops=0, bytes_accessed=2**18, transcendentals=0),
        name="collect",
    )(blocks, *pieces)


def dp_permute(value, dx, dz):
    pairs = []
    for source in range(8):
        x, z = source // 2, source % 2
        pairs.append((source, ((x + dx) % 4) * 2 + (z ^ dz)))
    return lax.ppermute(value, "dp", pairs)


def tensor_permute(value, dz, dy, dc):
    pairs = []
    for source in range(16):
        z, y, c = source // 8, (source // 2) % 4, source % 2
        pairs.append((source, (z ^ dz) * 8 + ((y + dy) % 4) * 2 + (c ^ dc)))
    return lax.ppermute(value, "tensor", pairs)


def tied(value, *after):
    return lax.optimization_barrier((value,) + after)[0]


def gather_output(shard, first, second, third):
    ring = tied(shard, *first)
    behind = dp_permute(ring, 1, 0)
    ahead = dp_permute(ring, 3, 0)
    other = dp_permute(tied(shard, *second), 0, 1)
    from_behind = dp_permute(jnp.concatenate([other, behind[:32]], axis=0), 1, 0)
    from_ahead = dp_permute(jnp.concatenate([other, ahead[32:]], axis=0), 3, 0)
    far_low = dp_permute(tied(from_behind, *third)[:32], 1, 0)
    far_high = dp_permute(tied(from_ahead, *third)[32:64], 3, 0)
    return shard, behind, ahead, other, from_behind, from_ahead, far_low, far_high


def on_device(
    qkv_master,
    qkv_moment1,
    qkv_moment2,
    qkv_grad,
    out_master,
    out_moment1,
    out_moment2,
    out_grad,
    embed_table,
    norm_gain,
    token_ids,
    lengths,
    kv_cache,
):
    group_rows, step_total = token_ids.shape
    my_group = lax.axis_index("dp")
    my_tensor = lax.axis_index("tensor")
    my_x, my_z = my_group // 2, my_group % 2
    my_core = my_tensor % 2

    ids_row = token_ids.reshape(1, TOK)
    new_qkv = adamw(qkv_master, qkv_moment1, qkv_moment2, qkv_grad)
    qkv_local = new_qkv[0].astype(bf16)[0]
    kept = lax.dynamic_slice(qkv_local, (0, my_core * HALF), (64, HALF))
    given = lax.dynamic_slice(qkv_local, (0, (1 - my_core) * HALF), (64, HALF))
    taken = tensor_permute(given, 0, 0, 1)
    new_out = adamw(out_master, out_moment1, out_moment2, out_grad)
    out_local = new_out[0].astype(bf16)[0]
    ids_sent = tied(jnp.broadcast_to(ids_row[None], (GROUPS, 1, TOK)), taken)
    all_ids = lax.all_to_all(ids_sent, "dp", split_axis=0, concat_axis=0, tiled=True)

    kept_z = dp_permute(kept, 0, 1)
    taken_z = dp_permute(taken, 0, 1)
    behind = dp_permute(taken, 1, 0)
    ahead = dp_permute(taken, 3, 0)
    up = jnp.concatenate([kept, kept_z, behind[:32]], axis=0)
    down = jnp.concatenate([kept, kept_z, ahead[32:]], axis=0)
    near = jnp.concatenate([behind, ahead], axis=0)
    from_behind = dp_permute(up, 1, 0)
    from_ahead = dp_permute(down, 3, 0)
    near_z = dp_permute(near, 0, 1)
    far = dp_permute(from_behind[:64], 1, 0)
    far_z = dp_permute(from_ahead[64:128], 3, 0)
    far_taken = jnp.concatenate([from_behind[128:160], from_ahead[128:160]], axis=0)
    far_taken_z = dp_permute(far_taken, 0, 1)
    qkv_pieces = (
        kept,
        kept_z,
        from_behind,
        from_ahead,
        far,
        far_z,
        taken,
        taken_z,
        behind,
        ahead,
        far_taken,
        near_z,
        far_taken_z,
    )

    table = embed_table.transpose(1, 2, 0).reshape(FEAT, VOCAB_DEV)
    sent = lookup(tied(all_ids, up, down, near), table)
    received = lax.all_to_all(
        sent.reshape(GROUPS, SLOTS, FEAT), "dp", split_axis=0, concat_axis=0, tiled=True
    ).reshape(GROUPS * SLOTS, FEAT)
    received = tied(received, far_taken, out_local)
    blocks = jnp.stack(
        [
            ((my_x + 4 - step) % 4) * 2 + (my_z + flip) % 2
            for flip in (0, 1)
            for step in (0, 1, 3, 2)
        ]
    )
    hidden, scaled, squares = arrange(all_ids, received, norm_gain)
    scaled_pair = tensor_permute(scaled, 0, 0, 1)

    cosine, sine = angles_of(lengths, step_total)
    partial = project(scaled, scaled_pair, squares, qkv_pieces)
    parts = lax.all_to_all(
        partial.reshape(16, 16, HALF + 128), "tensor", split_axis=0, concat_axis=0, tiled=True
    )
    attended, fresh_flat = attend(lengths, parts, cosine, sine, kv_cache)
    fresh_kv = fresh_flat.reshape(4, step_total, KVH, 2 * HD)

    other = tensor_permute(attended, 1, 0, 0)
    out_pieces = gather_output(out_local, (far, far_z, far_taken_z,), (far, far_z, far_taken_z,), (other,))
    both = jnp.stack([attended, other])
    quad = jnp.stack([both] + [tensor_permute(both, 0, step, 0) for step in (1, 2, 3)])
    away = tensor_permute(quad, 0, 0, 1)
    tensor_z, tensor_y = my_tensor // 8, (my_tensor // 2) % 4
    heads = jnp.zeros((16, 16, QW), bf16)
    for core, found in enumerate((quad, away)):
        for step in range(4):
            for flip in range(2):
                source = (
                    ((tensor_z + flip) % 2) * 8
                    + ((tensor_y + 4 - step) % 4) * 2
                    + (my_core + core) % 2
                )
                heads = lax.dynamic_update_slice(heads, found[step, flip][None], (source, 0, 0))
    output = lax.dot_general(
        heads.reshape(TOK, QW),
        collect(blocks.astype(jnp.int32), out_pieces),
        (((1,), (1,)), ((), ())),
        preferred_element_type=f32,
    )
    decoded = (hidden.astype(f32) + output).astype(bf16).reshape(group_rows, step_total, 8, 64)
    return (
        decoded,
        fresh_kv,
        new_qkv[0],
        new_qkv[1],
        new_qkv[2],
        new_out[0],
        new_out[1],
        new_out[2],
    )


def solution(mesh):
    return jax.shard_map(
        on_device,
        mesh=mesh,
        in_specs=(
            P("dp", "tensor", None),
            P("dp", "tensor", None),
            P("dp", "tensor", None),
            P("dp", "tensor", None),
            P("dp", "tensor", None),
            P("dp", "tensor", None),
            P("dp", "tensor", None),
            P("dp", "tensor", None),
            P("dp", None, "tensor"),
            P(None, "tensor"),
            P("dp", None),
            P(("dp", "tensor")),
            P(("dp", "tensor"), None, None, None),
        ),
        out_specs=(
            P("dp", None, None, "tensor"),
            P(("dp", "tensor"), None, None, None),
            P("dp", "tensor", None),
            P("dp", "tensor", None),
            P("dp", "tensor", None),
            P("dp", "tensor", None),
            P("dp", "tensor", None),
            P("dp", "tensor", None),
        ),
        check_vma=False,
    )
```

```python
import math

import jax
import jax.numpy as jnp
from jax import lax
from jax.experimental import pallas as pl
from jax.experimental.pallas import tpu as pltpu
from jax.sharding import PartitionSpec as P

D = 8192
QH = 32
KVH = 4
HD = 128
QW = 4096
KW = 512
VOCAB_DEV = 9504
SLOTS = 64
GROUPS = 8
TOK = 256
FEAT = 512
VCHUNK = 3200
HALF = 2560
COLS = 896
VMEM = 56 * 2**20

beta_first = 0.9
beta_second = 0.95
adam_epsilon = 1e-08
learn_rate = 0.002
decay_rate = 0.1
bias_first = 1.0 - 0.9**50
bias_second = 1.0 - 0.95**50
rope_base = 1000000.0
norm_epsilon = 1e-06

f32 = jnp.float32
bf16 = jnp.bfloat16


def adamw(master, moment_one, moment_two, gradient):
    grad_float = gradient.astype(jnp.float32)
    moment_one = beta_first * moment_one + (1.0 - beta_first) * grad_float
    moment_two = beta_second * moment_two + (1.0 - beta_second) * grad_float * grad_float
    stepped = moment_one / bias_first / (jnp.sqrt(moment_two / bias_second) + adam_epsilon)
    master = master - learn_rate * (stepped + decay_rate * master)
    return (master, moment_one, moment_two)


def iota(shape, axis):
    return lax.broadcasted_iota(jnp.int32, shape, axis)


def lower_triangle(size):
    return (iota((size, size), 0) <= iota((size, size), 1)).astype(bf16)


def lookup_kernel(ids_ref, table_ref, out_ref, acc_ref, pick_ref):
    step = pl.program_id(0)

    @pl.when(step == 0)
    def _():
        local = ids_ref[:, 0, :] - lax.axis_index("dp") * VOCAB_DEV
        mine = (local >= 0) & (local < VOCAB_DEV)
        rank = jnp.dot(
            mine.astype(f32).astype(bf16), lower_triangle(TOK), preferred_element_type=f32
        )
        rank = jnp.where(mine, rank, 0.0)
        shifted = local.astype(f32) + 1.0
        for group in range(GROUPS):
            slot = iota((SLOTS, TOK), 0).astype(f32) + 1.0
            hit = rank[group : group + 1, :] == slot
            value = jnp.where(hit, shifted[group : group + 1, :], 0.0)
            pick = jnp.sum(value, axis=1, keepdims=True) - 1.0
            pick_ref[pl.ds(group * SLOTS, SLOTS), :] = jnp.broadcast_to(
                pick, (SLOTS, 128)
            ).astype(jnp.int32)
        acc_ref[...] = jnp.zeros_like(acc_ref)

    slots = GROUPS * SLOTS
    entry = iota((slots, VCHUNK), 1) + step * VCHUNK
    chosen = jnp.where(entry == pick_ref[:, 0:1], 1.0, 0.0).astype(bf16)
    dims = (((1,), (1,)), ((), ()))

    @pl.when(step < pl.num_programs(0) - 1)
    def _():
        acc_ref[...] += lax.dot_general(chosen, table_ref[...], dims, preferred_element_type=f32)

    @pl.when(step == pl.num_programs(0) - 1)
    def _():
        column = iota((FEAT, VCHUNK), 1) + step * VCHUNK
        block = jnp.where(column < VOCAB_DEV, table_ref[...], jnp.zeros((), bf16))
        total = acc_ref[...] + lax.dot_general(chosen, block, dims, preferred_element_type=f32)
        out_ref[...] = total.astype(bf16)


def lookup(all_ids, table):
    steps = pl.cdiv(VOCAB_DEV, VCHUNK)
    slots = GROUPS * SLOTS
    return pl.pallas_call(
        lookup_kernel,
        grid=(steps,),
        in_specs=[
            pl.BlockSpec((GROUPS, 1, TOK), lambda i: (0, 0, 0)),
            pl.BlockSpec((FEAT, VCHUNK), lambda i: (0, i)),
        ],
        out_specs=pl.BlockSpec((slots, FEAT), lambda i: (0, 0)),
        out_shape=jax.ShapeDtypeStruct((slots, FEAT), bf16),
        scratch_shapes=[pltpu.VMEM((slots, FEAT), f32), pltpu.VMEM((slots, 128), jnp.int32)],
        compiler_params=pltpu.CompilerParams(vmem_limit_bytes=VMEM),
        cost_estimate=pl.CostEstimate(flops=3 * 10**10, bytes_accessed=10**7, transcendentals=0),
        name="lookup",
    )(all_ids, table)


def arrange_kernel(ids_ref, slots_ref, gain_ref, hidden_ref, scaled_ref, squares_ref):
    group = lax.axis_index("dp")
    ids = jnp.where(iota((GROUPS, TOK), 0) == group, ids_ref[:, 0, :], 0)
    ids = jnp.broadcast_to(jnp.sum(ids, axis=0, keepdims=True), (GROUPS, TOK))
    low = iota((GROUPS, TOK), 0) * VOCAB_DEV
    owned = (ids >= low) & (ids < low + VOCAB_DEV)
    rank = jnp.dot(owned.astype(f32).astype(bf16), lower_triangle(TOK), preferred_element_type=f32)
    place = rank - 1.0 + (iota((GROUPS, TOK), 0) * SLOTS).astype(f32)
    place = jnp.sum(jnp.where(owned, place, 0.0), axis=0, keepdims=True)
    slots = GROUPS * SLOTS
    chosen = jnp.where(iota((slots, TOK), 0).astype(f32) == place, 1.0, 0.0).astype(bf16)
    hidden = lax.dot_general(
        chosen, slots_ref[...], (((0,), (0,)), ((), ())), preferred_element_type=f32
    )
    hidden_ref[...] = hidden.astype(bf16)
    squares = jnp.sum(hidden * hidden, axis=1, keepdims=True)
    squares_ref[...] = jnp.broadcast_to(squares, (TOK, 128)).astype(bf16)
    gain = jnp.concatenate([gain_ref[block : block + 1, :] for block in range(8)], axis=1)
    scaled = (hidden * gain).astype(bf16)
    lane = iota((1, FEAT), 1)
    step = (lane // 64) % 4
    step = jnp.where(step == 2, 3, jnp.where(step == 3, 2, step))
    block = ((group // 2 + 4 - step) % 4) * 2 + (group % 2 + lane // 256) % 2
    order = block * 64 + lane % 64
    order = jnp.where(iota((FEAT, FEAT), 0) == order, 1.0, 0.0).astype(bf16)
    scaled_ref[...] = jnp.dot(scaled, order, preferred_element_type=f32).astype(bf16)


def arrange(all_ids, slots, gain):
    return pl.pallas_call(
        arrange_kernel,
        out_shape=(
            jax.ShapeDtypeStruct((TOK, FEAT), bf16),
            jax.ShapeDtypeStruct((TOK, FEAT), bf16),
            jax.ShapeDtypeStruct((TOK, 128), bf16),
        ),
        compiler_params=pltpu.CompilerParams(vmem_limit_bytes=VMEM),
        name="arrange",
    )(all_ids, slots, gain)


def project_kernel(own_ref, pair_ref, squares_ref, *rest):
    (
        first,
        first_z,
        from_behind,
        from_ahead,
        far,
        far_z,
        second,
        second_z,
        behind,
        ahead,
        far_second,
        near_z,
        far_second_z,
        out_ref,
    ) = rest
    own = jnp.concatenate(
        [
            first[...],
            from_behind[0:64, :],
            from_ahead[0:64, :],
            far[...],
            first_z[...],
            from_behind[64:128, :],
            from_ahead[64:128, :],
            far_z[...],
        ],
        axis=0,
    )
    pair = jnp.concatenate(
        [
            second[...],
            behind[...],
            ahead[...],
            far_second[...],
            second_z[...],
            near_z[...],
            far_second_z[...],
        ],
        axis=0,
    )
    total = jnp.dot(own_ref[...], own, preferred_element_type=f32)
    total = total + jnp.dot(pair_ref[...], pair, preferred_element_type=f32)
    out_ref[...] = total.astype(bf16)

    @pl.when(pl.program_id(0) == pl.num_programs(0) - 1)
    def _():
        out_ref[:, COLS - 128 : COLS] = squares_ref[...]


def project(own, pair, squares, shards):
    width = HALF + 128
    return pl.pallas_call(
        project_kernel,
        grid=(width // COLS,),
        in_specs=[
            pl.BlockSpec((TOK, FEAT), lambda i: (0, 0)),
            pl.BlockSpec((TOK, FEAT), lambda i: (0, 0)),
            pl.BlockSpec((TOK, 128), lambda i: (0, 0)),
        ]
        + [pl.BlockSpec((shard.shape[0], COLS), lambda i: (0, i)) for shard in shards],
        out_specs=pl.BlockSpec((TOK, COLS), lambda i: (0, i)),
        out_shape=jax.ShapeDtypeStruct((TOK, width), bf16),
        compiler_params=pltpu.CompilerParams(vmem_limit_bytes=VMEM),
        cost_estimate=pl.CostEstimate(
            flops=2 * TOK * 1024 * HALF, bytes_accessed=1024 * HALF * 2, transcendentals=0
        ),
        name="project",
    )(own, pair, squares, *shards)


def attend_kernel(
    lengths_ref, parts_ref, cos_ref, sin_ref, cache_ref, out_ref, fresh_ref, proj_ref
):
    head = pl.program_id(0)

    @pl.when(head == 0)
    def _():
        sums = []
        for core in range(2):
            total = parts_ref[core].astype(f32)
            for chip in range(1, 8):
                total = total + parts_ref[2 * chip + core].astype(f32)
            sums.append(total)
        squares = sums[0][:, HALF : HALF + 1] + sums[1][:, HALF : HALF + 1]
        inverse = lax.rsqrt(squares * (1.0 / D) + norm_epsilon)
        for core in range(2):
            proj_ref[:, core * HALF : (core + 1) * HALF] = sums[core][:, :HALF] * inverse

    cosine, sine = cos_ref[...], sin_ref[...]

    def turned(values):
        return (values * cosine + pltpu.roll(values, 64, 1) * sine).astype(bf16)

    def columns(first):
        return proj_ref[:, pl.ds(pl.multiple_of(first, 128), 128)]

    query = jnp.concatenate(
        [turned(columns(head * 1024 + group * 128)) for group in range(8)], axis=0
    )
    key_new = turned(columns(QW + head * 128))
    value_new = columns(QW + KW + head * 128).astype(bf16)
    fresh_ref[:, 0:128] = key_new
    fresh_ref[:, 128:256] = value_new

    scale = 1.0 / math.sqrt(HD)
    across = (((1,), (1,)), ((), ()))
    context = cache_ref.shape[2]
    token = iota((128, context), 0) % 16
    place = iota((128, context), 1)
    scores = []
    for row in range(4):
        score = (
            lax.dot_general(query, cache_ref[row, 0, :, :HD], across, preferred_element_type=f32)
            * scale
        )
        live = (token // 4 == row) & (place < lengths_ref[row])
        scores.append(jnp.where(live, score, -jnp.inf))
    score = lax.dot_general(query, key_new, across, preferred_element_type=f32) * scale
    asking, asked = iota((128, 16), 0) % 16, iota((128, 16), 1)
    live = (asking // 4 == asked // 4) & (asking % 4 >= asked % 4)
    scores.append(jnp.where(live, score, -jnp.inf))
    highest = jnp.max(scores[4], axis=1, keepdims=True)
    for score in scores[:4]:
        highest = jnp.maximum(highest, jnp.max(score, axis=1, keepdims=True))
    raised = [jnp.exp(score - highest) for score in scores]
    denom = jnp.sum(raised[4], axis=1, keepdims=True)
    for part in raised[:4]:
        denom = denom + jnp.sum(part, axis=1, keepdims=True)
    share = 1.0 / denom
    mixed = jnp.dot((raised[4] * share).astype(bf16), value_new, preferred_element_type=f32)
    for row in range(4):
        mixed = mixed + jnp.dot(
            (raised[row] * share).astype(bf16),
            cache_ref[row, 0, :, HD:],
            preferred_element_type=f32,
        )
    for group in range(8):
        out_ref[:, group * 128 : (group + 1) * 128] = mixed[group * 16 : (group + 1) * 16].astype(
            bf16
        )


def attend(lengths, parts, cosine, sine, cache):
    rows, heads, context, width = cache.shape
    return pl.pallas_call(
        attend_kernel,
        grid=(heads,),
        in_specs=[
            pl.BlockSpec(memory_space=pltpu.SMEM),
            pl.BlockSpec((16, 16, HALF + 128), lambda n: (0, 0, 0)),
            pl.BlockSpec((16, HD), lambda n: (0, 0)),
            pl.BlockSpec((16, HD), lambda n: (0, 0)),
            pl.BlockSpec((rows, 1, context, width), lambda n: (0, n, 0, 0)),
        ],
        out_specs=(
            pl.BlockSpec((16, 1024), lambda n: (0, n)),
            pl.BlockSpec((16, 256), lambda n: (0, n)),
        ),
        out_shape=(
            jax.ShapeDtypeStruct((16, QW), bf16),
            jax.ShapeDtypeStruct((16, 2 * KW), bf16),
        ),
        scratch_shapes=[pltpu.VMEM((16, 2 * HALF), f32)],
        compiler_params=pltpu.CompilerParams(vmem_limit_bytes=VMEM),
        name="attend",
    )(lengths, parts, cosine, sine, cache)


def angles_of(lengths, step_total):
    half_dim = HD // 2
    exponent = jnp.arange(half_dim).astype(f32) * (2.0 / HD)
    freqs = jnp.power(f32(rope_base), -exponent)
    positions = (lengths[:, None] + jnp.arange(step_total)[None, :]).reshape(-1)
    angles = positions.astype(f32)[:, None] * freqs
    cosine, sine = jnp.cos(angles), jnp.sin(angles)
    return jnp.concatenate([cosine, cosine], axis=1), jnp.concatenate([-sine, sine], axis=1)


OUT_PIECES = (
    (0, 0, 64, 0, 0),
    (1, 0, 64, 1, 0),
    (2, 0, 64, 2, 0),
    (4, 64, 32, 3, 0),
    (5, 64, 32, 3, 32),
    (3, 0, 64, 4, 0),
    (4, 0, 64, 5, 0),
    (5, 0, 64, 6, 0),
    (6, 0, 32, 7, 0),
    (7, 0, 32, 7, 32),
)


def collect_kernel(blocks_ref, *rest):
    pieces, (out_ref, sems) = rest[:8], rest[8:]
    copies = []
    for piece, first, count, block, offset in OUT_PIECES:
        row = pl.multiple_of(blocks_ref[block] * 64 + offset, 32)
        copies.append(
            pltpu.make_async_copy(
                pieces[piece].at[pl.ds(first, count), :],
                out_ref.at[pl.ds(row, count), :],
                sems.at[len(copies)],
            )
        )
    for copy in copies:
        copy.start()
    for copy in copies:
        copy.wait()


def collect(blocks, pieces):
    anywhere = pl.BlockSpec(memory_space=pl.ANY)
    return pl.pallas_call(
        collect_kernel,
        in_specs=[pl.BlockSpec(memory_space=pltpu.SMEM)] + [anywhere] * 8,
        out_specs=pl.BlockSpec(memory_space=pltpu.VMEM),
        out_shape=jax.ShapeDtypeStruct((FEAT, QW), bf16),
        scratch_shapes=[pltpu.SemaphoreType.DMA((len(OUT_PIECES),))],
        compiler_params=pltpu.CompilerParams(vmem_limit_bytes=16 * 2**20),
        cost_estimate=pl.CostEstimate(flops=0, bytes_accessed=2**18, transcendentals=0),
        name="collect",
    )(blocks, *pieces)


def dp_permute(value, dx, dz):
    pairs = []
    for source in range(8):
        x, z = source // 2, source % 2
        pairs.append((source, ((x + dx) % 4) * 2 + (z ^ dz)))
    return lax.ppermute(value, "dp", pairs)


def tensor_permute(value, dz, dy, dc):
    pairs = []
    for source in range(16):
        z, y, c = source // 8, (source // 2) % 4, source % 2
        pairs.append((source, (z ^ dz) * 8 + ((y + dy) % 4) * 2 + (c ^ dc)))
    return lax.ppermute(value, "tensor", pairs)


def tied(value, *after):
    return lax.optimization_barrier((value,) + after)[0]


def gather_output(shard, first, second, third):
    ring = tied(shard, *first)
    behind = dp_permute(ring, 1, 0)
    ahead = dp_permute(ring, 3, 0)
    other = dp_permute(tied(shard, *second), 0, 1)
    from_behind = dp_permute(jnp.concatenate([other, behind[:32]], axis=0), 1, 0)
    from_ahead = dp_permute(jnp.concatenate([other, ahead[32:]], axis=0), 3, 0)
    far_low = dp_permute(tied(from_behind, *third)[:32], 1, 0)
    far_high = dp_permute(tied(from_ahead, *third)[32:64], 3, 0)
    return shard, behind, ahead, other, from_behind, from_ahead, far_low, far_high


def on_device(
    qkv_master,
    qkv_moment1,
    qkv_moment2,
    qkv_grad,
    out_master,
    out_moment1,
    out_moment2,
    out_grad,
    embed_table,
    norm_gain,
    token_ids,
    lengths,
    kv_cache,
):
    group_rows, step_total = token_ids.shape
    my_group = lax.axis_index("dp")
    my_tensor = lax.axis_index("tensor")
    my_x, my_z = my_group // 2, my_group % 2
    my_core = my_tensor % 2

    ids_row = token_ids.reshape(1, TOK)
    new_qkv = adamw(qkv_master, qkv_moment1, qkv_moment2, qkv_grad)
    qkv_local = new_qkv[0].astype(bf16)[0]
    kept = lax.dynamic_slice(qkv_local, (0, my_core * HALF), (64, HALF))
    given = lax.dynamic_slice(qkv_local, (0, (1 - my_core) * HALF), (64, HALF))
    taken = tensor_permute(given, 0, 0, 1)
    new_out = adamw(out_master, out_moment1, out_moment2, out_grad)
    out_local = new_out[0].astype(bf16)[0]
    ids_sent = tied(jnp.broadcast_to(ids_row[None], (GROUPS, 1, TOK)), taken)
    all_ids = lax.all_to_all(ids_sent, "dp", split_axis=0, concat_axis=0, tiled=True)

    kept_z = dp_permute(kept, 0, 1)
    taken_z = dp_permute(taken, 0, 1)
    behind = dp_permute(taken, 1, 0)
    ahead = dp_permute(taken, 3, 0)
    up = jnp.concatenate([kept, kept_z, behind[:32]], axis=0)
    down = jnp.concatenate([kept, kept_z, ahead[32:]], axis=0)
    near = jnp.concatenate([behind, ahead], axis=0)
    from_behind = dp_permute(up, 1, 0)
    from_ahead = dp_permute(down, 3, 0)
    near_z = dp_permute(near, 0, 1)
    far = dp_permute(from_behind[:64], 1, 0)
    far_z = dp_permute(from_ahead[64:128], 3, 0)
    far_taken = jnp.concatenate([from_behind[128:160], from_ahead[128:160]], axis=0)
    far_taken_z = dp_permute(far_taken, 0, 1)
    qkv_pieces = (
        kept,
        kept_z,
        from_behind,
        from_ahead,
        far,
        far_z,
        taken,
        taken_z,
        behind,
        ahead,
        far_taken,
        near_z,
        far_taken_z,
    )

    table = embed_table.transpose(1, 2, 0).reshape(FEAT, VOCAB_DEV)
    sent = lookup(tied(all_ids, up, down, near), table)
    received = lax.all_to_all(
        sent.reshape(GROUPS, SLOTS, FEAT), "dp", split_axis=0, concat_axis=0, tiled=True
    ).reshape(GROUPS * SLOTS, FEAT)
    received = tied(received, out_local)
    blocks = jnp.stack(
        [
            ((my_x + 4 - step) % 4) * 2 + (my_z + flip) % 2
            for flip in (0, 1)
            for step in (0, 1, 3, 2)
        ]
    )
    hidden, scaled, squares = arrange(all_ids, received, norm_gain)
    scaled_pair = tensor_permute(scaled, 0, 0, 1)

    cosine, sine = angles_of(lengths, step_total)
    partial = project(scaled, scaled_pair, squares, qkv_pieces)
    parts = lax.all_to_all(
        partial.reshape(16, 16, HALF + 128), "tensor", split_axis=0, concat_axis=0, tiled=True
    )
    attended, fresh_flat = attend(lengths, parts, cosine, sine, kv_cache)
    fresh_kv = fresh_flat.reshape(4, step_total, KVH, 2 * HD)

    other = tensor_permute(attended, 1, 0, 0)
    out_pieces = gather_output(out_local, (far, far_z, far_taken_z,), (far, far_z, far_taken_z,), (other,))
    both = jnp.stack([attended, other])
    quad = jnp.stack([both] + [tensor_permute(both, 0, step, 0) for step in (1, 2, 3)])
    away = tensor_permute(quad, 0, 0, 1)
    tensor_z, tensor_y = my_tensor // 8, (my_tensor // 2) % 4
    heads = jnp.zeros((16, 16, QW), bf16)
    for core, found in enumerate((quad, away)):
        for step in range(4):
            for flip in range(2):
                source = (
                    ((tensor_z + flip) % 2) * 8
                    + ((tensor_y + 4 - step) % 4) * 2
                    + (my_core + core) % 2
                )
                heads = lax.dynamic_update_slice(heads, found[step, flip][None], (source, 0, 0))
    output = lax.dot_general(
        heads.reshape(TOK, QW),
        collect(blocks.astype(jnp.int32), out_pieces),
        (((1,), (1,)), ((), ())),
        preferred_element_type=f32,
    )
    decoded = (hidden.astype(f32) + output).astype(bf16).reshape(group_rows, step_total, 8, 64)
    return (
        decoded,
        fresh_kv,
        new_qkv[0],
        new_qkv[1],
        new_qkv[2],
        new_out[0],
        new_out[1],
        new_out[2],
    )


def solution(mesh):
    return jax.shard_map(
        on_device,
        mesh=mesh,
        in_specs=(
            P("dp", "tensor", None),
            P("dp", "tensor", None),
            P("dp", "tensor", None),
            P("dp", "tensor", None),
            P("dp", "tensor", None),
            P("dp", "tensor", None),
            P("dp", "tensor", None),
            P("dp", "tensor", None),
            P("dp", None, "tensor"),
            P(None, "tensor"),
            P("dp", None),
            P(("dp", "tensor")),
            P(("dp", "tensor"), None, None, None),
        ),
        out_specs=(
            P("dp", None, None, "tensor"),
            P(("dp", "tensor"), None, None, None),
            P("dp", "tensor", None),
            P("dp", "tensor", None),
            P("dp", "tensor", None),
            P("dp", "tensor", None),
            P("dp", "tensor", None),
            P("dp", "tensor", None),
        ),
        check_vma=False,
    )
```
